256 devices in a mesh: dp: 32 (over z, x_lo, core), tensor: 8 (over x_hi, y).
Axes of the slice: x: 4 (x_hi: 2, x_lo: 2; x = x_hi * 2 + x_lo), y: 4, z: 8, core: 2. Of those that a mesh axis runs over, the one named last changes fastest.
Arguments:
- tile_rows: bfloat16 [96, 256, 6144], P('dp', 'tensor'), may hold values from -6 to 6
- queries: bfloat16 [96, 256, 3072], P('dp', None, 'tensor'), may hold values from -6 to 6
- keys: bfloat16 [96, 256, 3072], P('dp', None, 'tensor'), may hold values from -6 to 6
- w_value: bfloat16 [6144, 3072], P(None, 'tensor'), may hold values from -0.078125 to 0.078125
- ctx_grad: bfloat16 [64, 256, 3072], P('dp', None, 'tensor'), may hold values from -6 to 6
- move: int32 [32, 3], replicated, may hold values from -1 to 63, as said below
- blocks: int32 [64, 256], P('dp'), may hold values from 0 to 3, never falling along the last dimension, each value on 1 to 128 neighbouring positions
Outputs:
- attended: bfloat16 [64, 256, 3072], P('dp', None, 'tensor')
- tile_grad: bfloat16 [96, 256, 6144], P('dp', 'tensor')
- query_grad: bfloat16 [96, 256, 3072], P('dp', None, 'tensor')
- key_grad: bfloat16 [96, 256, 3072], P('dp', None, 'tensor')
- weight_grad: float32 [6144, 3072], P('dp', 'tensor')
The draws below stay inside these ranges and needn't reach their ends.
Inputs may be any that keep to these rules, and one draw needn't show every extreme that they name: move[r, j] is the balanced slot r2 * 2 + i of home tile row j of data rank r, or -1 for an empty row. A live row j below 2 keeps slot j on its own rank; a live row from 2 on goes to the data rank 32/2 away; no balanced slot takes two rows.
All inputs are finite; a program needn't handle non-finite values.
Results may differ from the reference program's by a relative error of at most 0.029.
Values may be sent and summed in bfloat16 or wider, within the bound.
No kernel may reach another device: no remote copies, remote signals or barrier semaphores. Data moves between devices by JAX's collectives and lax.ppermute only.
A program may use at most 128 MiB of HBM per device.

```python
import math
import jax
import jax.numpy as jnp
import numpy as np
from jax import lax

D = 6144
HD = 128
HEADS = 24
TILE = 256
SEGS = 4
WORK = 2
HOME = 3
SEG_MOST = 128
N_DP = 32
N_TENSOR = 8


def draw_queries(key, part):
    key = jax.random.fold_in(key, 21)
    full_shape = (N_DP * HOME, TILE, HEADS * HD)
    return jnp.clip(jax.random.normal(key, full_shape, jnp.float32), -6.0, 6.0).astype(jnp.bfloat16)


def draw_keys(key, part):
    key = jax.random.fold_in(key, 22)
    full_shape = (N_DP * HOME, TILE, HEADS * HD)
    return jnp.clip(jax.random.normal(key, full_shape, jnp.float32), -6.0, 6.0).astype(jnp.bfloat16)


def draw_move(key, part):
    key = jax.random.fold_in(key, 5)
    half_ranks = N_DP // 2
    pair_kind = jax.random.randint(key, (half_ranks,), 0, 3)
    pair_kind = pair_kind.at[0].set(2).at[half_ranks - 1].set(2)
    heavy = jnp.concatenate([pair_kind == 0, pair_kind == 1])
    swapping = jnp.concatenate([pair_kind == 2, pair_kind == 2])
    rank_ids = jnp.arange(N_DP)
    partner = (rank_ids + half_ranks) % N_DP
    slot_ids = jnp.arange(HOME)
    kept_count = jnp.where(heavy, WORK, WORK - 1)
    staying = jnp.where(slot_ids[None, :] < kept_count[:, None], rank_ids[:, None] * WORK + slot_ids[None, :], -1)
    sends = heavy | swapping
    leaving = jnp.where(sends[:, None] & (slot_ids[None, :] == WORK), partner[:, None] * WORK + WORK - 1, -1)
    return jnp.where(slot_ids[None, :] < WORK, staying, leaving).astype(jnp.int32)


def spiked(entries, rng, source, target, parts, factor):
    owner, partner = [(jnp.arange(entries.shape[position]) // (entries.shape[position] // parts)).reshape([-1 if axis == position else 1 for axis in range(entries.ndim)]) for position in (source, target)]
    chosen = jax.random.permutation(rng, parts)[partner]
    strong = (owner == chosen) | (owner == (partner + parts // 2) % parts)
    return jnp.where(strong, factor * entries, entries)


def levels(stream_key, dims, split, least, high):
    loudness = 1.0
    for dim, blocks in split:
        heights = jax.random.uniform(jax.random.fold_in(jax.random.fold_in(stream_key, 6), dim), (blocks,), jnp.float32, least / len(split), high / len(split))
        loudness = loudness * jnp.repeat(jnp.exp(heights), dims[dim] // blocks).reshape((-1,) + (1,) * (len(dims) - 1 - dim))
    return loudness


def length_profile(count, total, reach, skew):
    weights = [(1 << 20) // math.isqrt(rank ** skew) + 1 for rank in range(2, count + 1)]
    spare, holding = total - reach - (count - 1), [1] * (count - 1)
    while spare > 0:
        candidates = [i for i in range(count - 1) if holding[i] < reach]
        whole, remaining = sum([weights[i] for i in candidates]), spare
        for i in candidates:
            extra = min(reach - holding[i], max(1, remaining * weights[i] // whole), spare)
            holding[i] = holding[i] + extra
            spare = spare - extra
    return np.array([reach] + holding)


def uneven(key, count, total, reach, skew):
    if count == 2:
        one = jax.random.randint(key, (), max(1, total - reach), min(reach, total - 1) + 1)
        return jnp.stack([one, total - one])
    lengths = jnp.asarray(length_profile(count, total, reach, skew), jnp.int32)
    pairs = (count - 1) // 2
    donor, sink = lengths[1:1 + 2 * pairs:2], lengths[2:2 + 2 * pairs:2]
    margin = jnp.minimum(donor - 1, reach - sink)
    moved = jax.random.randint(jax.random.fold_in(key, 1), (pairs,), 0, 1 << 20) % (margin + 1)
    lengths = lengths.at[1:1 + 2 * pairs:2].set(donor - moved).at[2:2 + 2 * pairs:2].set(sink + moved)
    return lengths[jax.random.permutation(jax.random.fold_in(key, 2), count)]


def normal_values(key, extent, deviation, bound, shards=(), held_as=jnp.bfloat16):
    drawn = jax.random.normal(key, extent, jnp.float32) * deviation
    if len(shards) > 0:
        drawn = levels(key, extent, shards, -0.22, 0.18) * drawn
    return jnp.clip(drawn, min=-bound, max=bound).astype(held_as)


def noise_with(rng, extent, scale, bound, shards, heavy, kind=jnp.bfloat16):
    array = scale * jax.random.normal(rng, extent, jnp.float32)
    if shards:
        array = array * levels(rng, extent, shards, -0.22, 0.18)
    return jnp.clip(spiked(array, jax.random.fold_in(rng, 3), *heavy), -bound, bound).astype(kind)


def setup_inputs(seed: int = 0) -> dict:
    seeds = jax.random.split(jax.random.key(seed), 8)
    tile_rows = noise_with(seeds[0], (N_DP * HOME, TILE, D), 1.0, 6.0, ((0, 32), (1, 8)), (0, 2, 32, 2.75))
    queries = draw_queries(jax.random.fold_in(seeds[7], 71), 0)
    keys = draw_keys(jax.random.fold_in(seeds[7], 71), 0)
    w_value = normal_values(seeds[3], (D, HEADS * HD), D ** -0.5, 0.078125, ((1, 8),))
    ctx_grad = normal_values(seeds[4], (N_DP * WORK, TILE, HEADS * HD), 1.0, 6.0, ((0, 32), (2, 8)))
    move = draw_move(jax.random.fold_in(seeds[7], 71), 0)
    blocks = jax.vmap(lambda own: jnp.searchsorted(jnp.cumsum(uneven(own, SEGS, TILE, SEG_MOST, 2)), jnp.arange(TILE), side="right"))(jax.random.split(seeds[6], (N_DP * WORK))).reshape((N_DP * WORK, TILE)).astype(jnp.int32)
    return dict(tile_rows=tile_rows, queries=queries, keys=keys, w_value=w_value, ctx_grad=ctx_grad, move=move, blocks=blocks)


masked_score = -1e+30

def attention_weights(query_heads, key_heads, block_ids):
    score_scale = 1.0 / math.sqrt(HD)
    scores = jnp.einsum('qhd,khd->hqk', query_heads, key_heads) * score_scale
    same_block = block_ids[None, :, None] == block_ids[None, None, :]
    scores = jnp.where(same_block, scores, masked_score)
    row_max = lax.optimization_barrier(jnp.max(scores, axis=-1, keepdims=True))
    raised = jnp.exp(scores - row_max)
    return raised / lax.optimization_barrier(jnp.sum(raised, axis=-1, keepdims=True))

def tile_pass(rows, query_rows, key_rows, grad_rows, block_ids, w_value):
    tile_len = rows.shape[0]
    score_scale = 1.0 / math.sqrt(HD)
    values_low = lax.optimization_barrier(jnp.dot(rows, w_value, preferred_element_type=jnp.float32).astype(jnp.bfloat16))
    query_heads = query_rows.astype(jnp.float32).reshape(tile_len, HEADS, HD)
    key_heads = key_rows.astype(jnp.float32).reshape(tile_len, HEADS, HD)
    value_heads = values_low.astype(jnp.float32).reshape(tile_len, HEADS, HD)
    grad_heads = grad_rows.astype(jnp.float32).reshape(tile_len, HEADS, HD)
    probs = attention_weights(query_heads, key_heads, block_ids)
    probs_low = lax.optimization_barrier(probs.astype(jnp.bfloat16))
    probs_back = probs_low.astype(jnp.float32)
    attended = jnp.einsum('hqk,khd->qhd', probs_back, value_heads).astype(jnp.bfloat16).reshape(tile_len, HEADS * HD)
    prob_grad = jnp.einsum('qhd,khd->hqk', grad_heads, value_heads)
    value_grad = jnp.einsum('hqk,qhd->khd', probs_back, grad_heads).astype(jnp.bfloat16).reshape(tile_len, HEADS * HD)
    inner_sum = lax.optimization_barrier(jnp.sum(prob_grad * probs, axis=-1, keepdims=True))
    score_low = lax.optimization_barrier((probs * (prob_grad - inner_sum) * score_scale).astype(jnp.bfloat16))
    score_grad = score_low.astype(jnp.float32)
    query_grad = jnp.einsum('hqk,khd->qhd', score_grad, key_heads).astype(jnp.bfloat16).reshape(tile_len, HEADS * HD)
    key_grad = jnp.einsum('hqk,qhd->khd', score_grad, query_heads).astype(jnp.bfloat16).reshape(tile_len, HEADS * HD)
    group_width = HEADS * HD // N_TENSOR
    row_total = jnp.zeros((tile_len, D), jnp.float32)
    for group_index in range(N_TENSOR):
        first_col = group_index * group_width
        last_col = first_col + group_width
        partial_rows = jnp.dot(value_grad[:, first_col:last_col], w_value[:, first_col:last_col].T, preferred_element_type=jnp.float32)
        partial_low = lax.optimization_barrier(partial_rows.astype(jnp.bfloat16))
        row_total = row_total + partial_low.astype(jnp.float32)
    row_grad = row_total.astype(jnp.bfloat16)
    weight_term = jnp.dot(rows.T, value_grad, preferred_element_type=jnp.float32)
    return (weight_term, (attended, row_grad, query_grad, key_grad))

def reference(tile_rows, queries, keys, w_value, ctx_grad, move, blocks):
    slot_total = N_DP * WORK
    flat_move = move.reshape(-1).astype(jnp.int32)
    live_rows = flat_move >= 0
    target = jnp.where(live_rows, flat_move, slot_total).astype(jnp.int32)

    def spread(home_array):
        room = jnp.zeros((slot_total + 1,) + home_array.shape[1:], home_array.dtype)
        return room.at[target].set(home_array)[:slot_total]
    rows_bal = spread(tile_rows)
    queries_bal = spread(queries)
    keys_bal = spread(keys)

    def step_tile(total, pieces):
        rows, query_rows, key_rows, grad_rows, block_ids = pieces
        weight_term, results = tile_pass(rows, query_rows, key_rows, grad_rows, block_ids, w_value)
        return (total + weight_term, results)
    start_total = jnp.zeros((D, HEADS * HD), jnp.float32)
    weight_grad, results = lax.scan(step_tile, start_total, (rows_bal, queries_bal, keys_bal, ctx_grad, blocks))
    attended, rows_grad_bal, query_bal_grad, key_bal_grad = results
    source = jnp.where(live_rows, flat_move, 0).astype(jnp.int32)

    def bring_home(balanced):
        picked = balanced[source]
        return jnp.where(live_rows[:, None, None], picked, jnp.zeros_like(picked))
    return (attended, bring_home(rows_grad_bal), bring_home(query_bal_grad), bring_home(key_bal_grad), weight_grad)
```

```python
import functools
import math

import jax
import jax.numpy as jnp
from jax import lax
from jax.experimental import pallas as pl
from jax.experimental.pallas import tpu as pltpu
from jax.sharding import PartitionSpec as P

HD = 128
N_TENSOR = 8
N_Z = 8
masked_score = -1e30
BF = jnp.bfloat16
F32 = jnp.float32
VMEM_LIMIT = 48 * 1024 * 1024


def swap(x, d):
    return lax.ppermute(x, "tensor", [(i, i ^ d) for i in range(N_TENSOR)])


def dp_perm(x, move):
    pairs = []
    for z in range(N_Z):
        for xl in range(2):
            for c in range(2):
                z2, xl2, c2 = move(z, xl, c)
                pairs.append(((z * 2 + xl) * 2 + c, ((z2 % N_Z) * 2 + xl2 % 2) * 2 + c2 % 2))
    return lax.ppermute(x, "dp", pairs)


def to_partner(x):
    return dp_perm(x, lambda z, xl, c: (z + N_Z // 2, xl, c))


def along_z(x, by):
    return dp_perm(x, lambda z, xl, c: (z + by, xl, c))


def other_core(x):
    return dp_perm(x, lambda z, xl, c: (z, xl, c + 1))


def other_xl(x):
    return dp_perm(x, lambda z, xl, c: (z, xl + 1, c))


def gather_chunks(own, a, b):
    c = [None] * N_TENSOR
    c[0] = own
    c[4] = swap(own, 4)
    c[a] = swap(own, a)
    c[b] = swap(own, b)
    c[4 ^ b] = swap(c[b], 4)
    c[2] = swap(c[a], b)
    c[4 ^ a] = swap(c[4], a)
    c[6] = swap(c[4 ^ b], a)
    return c


def scatter_chunks(t, a, b):
    u4b = t[4 ^ b] + swap(t[6], a)
    ua = t[a] + swap(t[2], b)
    u4 = t[4] + swap(t[4 ^ a], a)
    ub = t[b] + swap(u4b, 4)
    parts = (t[0], swap(u4, 4), swap(ua, a), swap(ub, b))
    return sum(p.astype(F32) for p in parts).astype(BF)


def value_kernel(*refs):
    chunks, w_ref, out_ref, acc = refs[:8], refs[8], refs[9], refs[10]
    step = pl.program_id(0)
    rows = jnp.concatenate([c[...] for c in chunks], axis=0)
    part = jnp.dot(rows, w_ref[...], preferred_element_type=F32)

    @pl.when(step == 0)
    def _():
        acc[...] = part

    @pl.when(step > 0)
    def _():
        acc[...] += part

    @pl.when(step == pl.num_programs(0) - 1)
    def _():
        out_ref[...] = acc[...].astype(BF)


def project_values(chunks, w):
    n, d = chunks[0].shape
    cols = w.shape[1]
    blk = 1024
    return pl.pallas_call(
        value_kernel,
        grid=(d // blk,),
        in_specs=[pl.BlockSpec((n, blk), lambda i: (0, i))] * 8
        + [pl.BlockSpec((blk, cols), lambda i: (i, 0))],
        out_specs=pl.BlockSpec((8 * n, cols), lambda i: (0, 0)),
        out_shape=jax.ShapeDtypeStruct((8 * n, cols), BF),
        scratch_shapes=[pltpu.VMEM((8 * n, cols), F32)],
        compiler_params=pltpu.CompilerParams(vmem_limit_bytes=VMEM_LIMIT),
        cost_estimate=pl.CostEstimate(
            flops=2 * 8 * n * d * cols, bytes_accessed=2 * d * (8 * n + cols), transcendentals=0
        ),
        name="project_values",
    )(*chunks, w)


def attend_kernel(me_ref, q_ref, k_ref, v_ref, g_ref, bq_ref, bk_ref,
                  att_ref, vg_ref, dq_ref, dk_ref, v_abs, vg_abs):
    me = me_ref[0]
    n = q_ref.shape[0] // N_TENSOR
    scale = 1.0 / math.sqrt(HD)
    for d in range(N_TENSOR):
        at = pl.multiple_of((me ^ d) * n, n)
        v_abs[pl.ds(at, n), :] = v_ref[d * n:(d + 1) * n, :]
    q, k, g, v = q_ref[...], k_ref[...], g_ref[...], v_abs[...]
    nt = (((1,), (1,)), ((), ()))
    tn = (((0,), (0,)), ((), ()))
    s = lax.dot_general(q, k, nt, preferred_element_type=F32) * scale
    s = jnp.where(bq_ref[...] == bk_ref[...], s, masked_score)
    e = jnp.exp(s - jnp.max(s, axis=-1, keepdims=True))
    p = e / jnp.sum(e, axis=-1, keepdims=True)
    low = p.astype(BF)
    att_ref[...] = jnp.dot(low, v, preferred_element_type=F32).astype(BF)
    pg = lax.dot_general(g, v, nt, preferred_element_type=F32)
    vg_abs[...] = lax.dot_general(low, g, tn, preferred_element_type=F32).astype(BF)
    inner = jnp.sum(pg * p, axis=-1, keepdims=True)
    sg = (p * (pg - inner) * scale).astype(BF)
    dq_ref[...] = jnp.dot(sg, k, preferred_element_type=F32).astype(BF)
    dk_ref[...] = lax.dot_general(sg, q, tn, preferred_element_type=F32).astype(BF)
    for d in range(N_TENSOR):
        at = pl.multiple_of((me ^ d) * n, n)
        vg_ref[d * n:(d + 1) * n, :] = vg_abs[pl.ds(at, n), :]


def attend(me, q, k, v_rel, g, block_ids):
    t, cols = q.shape
    head = pl.BlockSpec((t, HD), lambda h, m: (0, h))
    return pl.pallas_call(
        attend_kernel,
        grid_spec=pltpu.PrefetchScalarGridSpec(
            num_scalar_prefetch=1,
            grid=(cols // HD,),
            in_specs=[head] * 4
            + [
                pl.BlockSpec((t, 1), lambda h, m: (0, 0)),
                pl.BlockSpec((1, t), lambda h, m: (0, 0)),
            ],
            out_specs=[head] * 4,
            scratch_shapes=[pltpu.VMEM((t, HD), BF)] * 2,
        ),
        out_shape=[jax.ShapeDtypeStruct((t, cols), BF)] * 4,
        compiler_params=pltpu.CompilerParams(vmem_limit_bytes=VMEM_LIMIT),
        cost_estimate=pl.CostEstimate(
            flops=12 * t * t * cols, bytes_accessed=16 * t * cols, transcendentals=3 * t * t
        ),
        name="attend",
    )(me, q, k, v_rel, g, block_ids.reshape(t, 1), block_ids.reshape(1, t))


def terms_kernel(vg_ref, w_ref, *outs):
    n = outs[0].shape[0]
    part = lax.dot_general(
        vg_ref[...], w_ref[...], (((1,), (1,)), ((), ())), preferred_element_type=F32
    ).astype(BF)
    for d in range(N_TENSOR):
        outs[d][...] = part[d * n:(d + 1) * n]


def row_terms(vg_rel, w):
    t, cols = vg_rel.shape
    d = w.shape[0]
    n = t // N_TENSOR
    blk = 1024
    return pl.pallas_call(
        terms_kernel,
        grid=(d // blk,),
        in_specs=[
            pl.BlockSpec((t, cols), lambda i: (0, 0)),
            pl.BlockSpec((blk, cols), lambda i: (i, 0)),
        ],
        out_specs=[pl.BlockSpec((n, blk), lambda i: (0, i))] * N_TENSOR,
        out_shape=[jax.ShapeDtypeStruct((n, d), BF)] * N_TENSOR,
        compiler_params=pltpu.CompilerParams(vmem_limit_bytes=VMEM_LIMIT),
        cost_estimate=pl.CostEstimate(
            flops=2 * t * d * cols, bytes_accessed=2 * d * (t + cols), transcendentals=0
        ),
        name="row_terms",
    )(vg_rel, w)


def weight_kernel(where_ref, *refs):
    chunks, vga_ref, vgb_ref, keep_ref, send_ref = refs[:16], refs[16], refs[17], refs[18], refs[19]
    rows = jnp.concatenate([c[...] for c in chunks], axis=0)
    vg = jnp.concatenate([vga_ref[...], vgb_ref[...]], axis=0)
    part = lax.dot_general(rows, vg, (((0,), (0,)), ((), ())), preferred_element_type=F32)
    part = part.astype(BF)
    half = part.shape[0] // 2
    mine = where_ref[1] == 0
    keep_ref[0] = jnp.where(mine, part[:half], part[half:])
    send_ref[0] = jnp.where(mine, part[half:], part[:half])


def weight_terms(where, chunks, vg_a, vg_b):
    n, d = chunks[0].shape
    t, cols = vg_a.shape
    blk = d // 16
    full = pl.BlockSpec((t, cols), lambda i, wh: (0, 0))
    out = pl.BlockSpec((1, blk // 2, cols), lambda i, wh: (i, 0, 0))
    return pl.pallas_call(
        weight_kernel,
        grid_spec=pltpu.PrefetchScalarGridSpec(
            num_scalar_prefetch=1,
            grid=(16,),
            in_specs=[
                pl.BlockSpec((n, blk), lambda i, wh: (0, lax.rem(wh[0] * 2 + i, 16)))
            ] * 16 + [full, full],
            out_specs=[out, out],
        ),
        out_shape=[jax.ShapeDtypeStruct((16, blk // 2, cols), BF)] * 2,
        compiler_params=pltpu.CompilerParams(vmem_limit_bytes=VMEM_LIMIT),
        cost_estimate=pl.CostEstimate(
            flops=2 * 2 * t * d * cols, bytes_accessed=2 * d * (2 * t + cols), transcendentals=0
        ),
        name="weight_terms",
    )(where, *chunks, vg_a, vg_b)


def weight_sum(keep, sent, xl):
    got = other_core(sent)
    u = keep + got
    u = [u[2 * i:2 * i + 2] for i in range(N_Z)]
    up = along_z(u[4][:1], 1)
    down = along_z(u[4][1:], -1)
    up = along_z(jnp.concatenate([u[3][:1] + up, u[3][1:]], axis=0), 1)
    down = along_z(jnp.concatenate([u[5][:1], u[5][1:] + down], axis=0), -1)
    up = along_z(u[2] + up, 1)
    down = along_z(u[6] + down, -1)
    up = along_z(u[1] + up, 1)
    down = along_z(u[7] + down, -1)
    total = u[0].astype(F32) + up.astype(F32) + down.astype(F32)
    mine = lax.dynamic_index_in_dim(total, xl, 0, keepdims=False)
    theirs = lax.dynamic_index_in_dim(total, 1 - xl, 0, keepdims=False)
    return mine + other_xl(theirs.astype(BF)).astype(F32)


def shards(tile_rows, queries, keys, w_value, ctx_grad, move, blocks):
    rank_count = lax.axis_size("dp")
    half_ranks = rank_count // 2
    my_rank = lax.axis_index("dp")
    partner = (my_rank + half_ranks) % rank_count
    me = lax.axis_index("tensor").astype(jnp.int32).reshape(1)
    z, xl, core = my_rank // 4, (my_rank // 2) % 2, my_rank % 2
    where = jnp.stack([z, core]).astype(jnp.int32)

    own_dest = move[my_rank]
    live = own_dest[:2] == my_rank * 2 + jnp.arange(2, dtype=jnp.int32)
    leaving = (own_dest[2] >= 0) & (own_dest[2] // 2 == partner)
    sender_dest = move[partner, 2]
    arriving = (sender_dest >= 0) & (sender_dest // 2 == my_rank)
    slot_b = jnp.where(arriving, sender_dest % 2, jnp.where(live[0], 1, 0)).astype(jnp.int32)
    slot_a = 1 - slot_b
    live_a, live_b = live[slot_a], live[slot_b]

    def own(home, slot):
        return lax.dynamic_index_in_dim(home, slot, 0, keepdims=False)

    def kept(home):
        row = own(home, slot_a)
        return jnp.where(live_a, row, jnp.zeros_like(row))

    def second(home, got):
        row = own(home, slot_b)
        return jnp.where(arriving, got, jnp.where(live_b, row, jnp.zeros_like(row)))

    got_rows = to_partner(tile_rows[2])
    rows_a = gather_chunks(kept(tile_rows), 1, 3)
    rows_b = gather_chunks(second(tile_rows, got_rows), 3, 1)
    late_q, late_k, _ = lax.optimization_barrier((queries[2], keys[2], got_rows))
    q_b, k_b = second(queries, to_partner(late_q)), second(keys, to_partner(late_k))
    q_a, k_a = kept(queries), kept(keys)

    values_a = project_values(rows_a, w_value)
    att_a, vg_a, dq_a, dk_a = attend(
        me, q_a, k_a, values_a, own(ctx_grad, slot_a), own(blocks, slot_a))
    values_b = project_values(rows_b, w_value)
    att_b, vg_b, dq_b, dk_b = attend(
        me, q_b, k_b, values_b, own(ctx_grad, slot_b), own(blocks, slot_b))

    grad_b = scatter_chunks(row_terms(vg_b, w_value), 3, 1)
    grad_a = scatter_chunks(row_terms(vg_a, w_value), 1, 3)
    keep, sent = weight_terms(where, rows_a + rows_b, vg_a, vg_b)
    weight_grad = weight_sum(keep, sent, xl)

    def by_slot(of_a, of_b):
        first = slot_a == 0
        return [jnp.where(first, of_a, of_b), jnp.where(first, of_b, of_a)]

    def home(of_a, of_b):
        back = to_partner(of_b)
        here = by_slot(of_a, of_b)
        rows = [jnp.where(live[0], here[0], 0), jnp.where(live[1], here[1], 0),
                jnp.where(leaving, back, 0)]
        return jnp.stack(rows).astype(BF)

    attended = jnp.stack(by_slot(att_a, att_b))
    return (attended, home(grad_a, grad_b), home(dq_a, dq_b), home(dk_a, dk_b), weight_grad)


def solution(mesh):
    placed = (
        P("dp", "tensor", None),
        P("dp", None, "tensor"),
        P("dp", None, "tensor"),
        P(None, "tensor"),
        P("dp", None, "tensor"),
        P(),
        P("dp", None),
    )
    return jax.shard_map(
        shards,
        mesh=mesh,
        in_specs=placed,
        out_specs=(
            P("dp", None, "tensor"),
            P("dp", "tensor", None),
            P("dp", None, "tensor"),
            P("dp", None, "tensor"),
            P("dp", "tensor"),
        ),
        check_vma=False,
    )
```

```python
import functools
import math

import jax
import jax.numpy as jnp
from jax import lax
from jax.experimental import pallas as pl
from jax.experimental.pallas import tpu as pltpu
from jax.sharding import PartitionSpec as P

HD = 128
N_TENSOR = 8
N_Z = 8
masked_score = -1e30
BF = jnp.bfloat16
F32 = jnp.float32
VMEM_LIMIT = 8 * 1024 * 1024
BLK = 1024
SMALL = pl.CostEstimate(flops=1, bytes_accessed=1, transcendentals=0)


def swap(x, d):
    return lax.ppermute(x, "tensor", [(i, i ^ d) for i in range(N_TENSOR)])


def dp_perm(x, move):
    pairs = []
    for z in range(N_Z):
        for xl in range(2):
            for c in range(2):
                z2, xl2, c2 = move(z, xl, c)
                pairs.append(((z * 2 + xl) * 2 + c, ((z2 % N_Z) * 2 + xl2 % 2) * 2 + c2 % 2))
    return lax.ppermute(x, "dp", pairs)


def to_partner(x):
    return dp_perm(x, lambda z, xl, c: (z + N_Z // 2, xl, c))


def along_z(x, by):
    return dp_perm(x, lambda z, xl, c: (z + by, xl, c))


def other_core(x):
    return dp_perm(x, lambda z, xl, c: (z, xl, c + 1))


def other_xl(x):
    return dp_perm(x, lambda z, xl, c: (z, xl + 1, c))


def gather_chunks(own, a, b):
    c = [None] * N_TENSOR
    c[0] = own
    c[4] = swap(own, 4)
    c[a] = swap(own, a)
    c[b] = swap(own, b)
    c[4 ^ b] = swap(c[b], 4)
    c[2] = swap(c[a], b)
    c[4 ^ a] = swap(c[4], a)
    c[6] = swap(c[4 ^ b], a)
    return c


def scatter_first(t, a, b, add_up):
    return (add_up(t[4 ^ b], swap(t[6], a)), add_up(t[a], swap(t[2], b)),
            add_up(t[4], swap(t[4 ^ a], a)))


def scatter_next(t, first, b):
    return t[b] + swap(first[0], 4)


def scatter_last(t, first, ub, a, b):
    _, ua, u4 = first
    parts = (t[0], swap(u4, 4), swap(ua, a), swap(ub, b))
    return sum(p.astype(F32) for p in parts).astype(BF)


VM = pl.BlockSpec(memory_space=pltpu.VMEM)
ANY = pl.BlockSpec(memory_space=pl.ANY)


def pack_kernel(n, *refs):
    for i in range(n):
        refs[-1][i] = refs[i][0]


def pack(homes, slot, after=()):
    _, t, cols = homes[0].shape
    n = len(homes)
    last = pl.BlockSpec((1, t, cols), lambda i: (slot, 0, 0))
    return pl.pallas_call(
        functools.partial(pack_kernel, n),
        grid=(1,),
        in_specs=[last] * n + [ANY] * len(after),
        out_specs=pl.BlockSpec((n, t, cols), lambda i: (0, 0, 0)),
        out_shape=jax.ShapeDtypeStruct((n, t, cols), BF),
        compiler_params=pltpu.CompilerParams(vmem_limit_bytes=VMEM_LIMIT),
        cost_estimate=SMALL,
        name="pack",
    )(*homes, *after)


def add_kernel(a_ref, b_ref, *refs):
    refs[-1][...] = a_ref[...] + b_ref[...]


def add(a, b, after):
    flat = a.ndim == 2
    blk = VM if flat else pl.BlockSpec((1,) + a.shape[1:], lambda i: (i, 0, 0))
    return pl.pallas_call(
        add_kernel,
        grid=() if flat else (a.shape[0],),
        in_specs=[blk, blk] + [ANY] * len(after),
        out_specs=blk,
        out_shape=jax.ShapeDtypeStruct(a.shape, a.dtype),
        compiler_params=pltpu.CompilerParams(vmem_limit_bytes=VMEM_LIMIT),
        cost_estimate=SMALL,
        name="add",
    )(a, b, *after)


def value_kernel(*refs):
    chunks, w_ref, out_ref = refs[:8], refs[8], refs[-1]
    d = w_ref.shape[0]
    acc = jnp.zeros(out_ref.shape, F32)
    for at in range(0, d, BLK):
        rows = jnp.concatenate([c[:, at:at + BLK] for c in chunks], axis=0)
        acc += jnp.dot(rows, w_ref[at:at + BLK, :], preferred_element_type=F32)
    out_ref[...] = acc.astype(BF)


def project_values(chunks, w, after=()):
    n, d = chunks[0].shape
    cols = w.shape[1]
    return pl.pallas_call(
        value_kernel,
        in_specs=[VM] * 9 + [ANY] * len(after),
        out_specs=VM,
        out_shape=jax.ShapeDtypeStruct((8 * n, cols), BF),
        compiler_params=pltpu.CompilerParams(vmem_limit_bytes=VMEM_LIMIT),
        cost_estimate=SMALL,
        name="project_values",
    )(*chunks, w, *after)


def attend_kernel(arrived, me_ref, *refs):
    q_ref, k_ref, v_ref, g_ref, bq_ref, bk_ref = refs[:6]
    got_ref = refs[6] if arrived else None
    att_ref, vg_ref, vgt_ref, dqk_ref, v_abs, vg_abs = refs[-6:]
    me, live, came = me_ref[0], me_ref[2] == 1, me_ref[3] == 1
    n = q_ref.shape[0] // N_TENSOR
    scale = 1.0 / math.sqrt(HD)
    for d in range(N_TENSOR):
        at = pl.multiple_of((me ^ d) * n, n)
        v_abs[pl.ds(at, n), :] = v_ref[d * n:(d + 1) * n, :]
    g, v = g_ref[...], v_abs[...]
    q = jnp.where(live, q_ref[...], 0).astype(BF)
    k = jnp.where(live, k_ref[...], 0).astype(BF)
    if arrived:
        q = jnp.where(came, got_ref[0], q)
        k = jnp.where(came, got_ref[1], k)
    nt = (((1,), (1,)), ((), ()))
    tn = (((0,), (0,)), ((), ()))
    s = lax.dot_general(q, k, nt, preferred_element_type=F32) * scale
    s = jnp.where(bq_ref[...] == bk_ref[...], s, masked_score)
    e = jnp.exp(s - jnp.max(s, axis=-1, keepdims=True))
    p = e / jnp.sum(e, axis=-1, keepdims=True)
    low = p.astype(BF)
    att_ref[...] = jnp.dot(low, v, preferred_element_type=F32).astype(BF)
    pg = lax.dot_general(g, v, nt, preferred_element_type=F32)
    vg_abs[...] = lax.dot_general(low, g, tn, preferred_element_type=F32).astype(BF)
    inner = jnp.sum(pg * p, axis=-1, keepdims=True)
    sg = (p * (pg - inner) * scale).astype(BF)
    dqk_ref[0] = jnp.dot(sg, k, preferred_element_type=F32).astype(BF)
    dqk_ref[1] = lax.dot_general(sg, q, tn, preferred_element_type=F32).astype(BF)
    vg = jnp.concatenate(
        [vg_abs[pl.ds(pl.multiple_of((me ^ d) * n, n), n), :] for d in range(N_TENSOR)], axis=0)
    vg_ref[...] = vg
    vgt_ref[...] = vg.T


def attend(info, q_home, k_home, v_rel, g, blocks, got=None, after=()):
    _, t, cols = q_home.shape
    row = pl.BlockSpec((None, t, HD), lambda h, m: (m[1], 0, h))
    flat = pl.BlockSpec((t, HD), lambda h, m: (0, h))
    two = pl.BlockSpec((2, t, HD), lambda h, m: (0, 0, h))
    arrived = got is not None
    shape = jax.ShapeDtypeStruct
    return pl.pallas_call(
        functools.partial(attend_kernel, arrived),
        grid_spec=pltpu.PrefetchScalarGridSpec(
            num_scalar_prefetch=1,
            grid=(cols // HD,),
            in_specs=[row, row, flat, row]
            + [
                pl.BlockSpec((None, t, 1), lambda h, m: (m[1], 0, 0)),
                pl.BlockSpec((None, 1, t), lambda h, m: (m[1], 0, 0)),
            ]
            + [two] * arrived + [ANY] * len(after),
            out_specs=[flat, flat, pl.BlockSpec((HD, t), lambda h, m: (h, 0)), two],
            scratch_shapes=[pltpu.VMEM((t, HD), BF)] * 2,
        ),
        out_shape=[shape((t, cols), BF), shape((t, cols), BF), shape((cols, t), BF),
                   shape((2, t, cols), BF)],
        compiler_params=pltpu.CompilerParams(vmem_limit_bytes=VMEM_LIMIT),
        cost_estimate=SMALL,
        name="attend",
    )(info, q_home, k_home, v_rel, g, blocks[:, :, None], blocks[:, None, :],
      *([got] if arrived else []), *after)


def terms_kernel(vg_ref, w_ref, *refs):
    outs = refs[-N_TENSOR:]
    n = outs[0].shape[0]
    for at in range(0, w_ref.shape[0], BLK):
        part = lax.dot_general(
            vg_ref[...], w_ref[at:at + BLK, :], (((1,), (1,)), ((), ())),
            preferred_element_type=F32,
        ).astype(BF)
        for d in range(N_TENSOR):
            outs[d][:, at:at + BLK] = part[d * n:(d + 1) * n]


def row_terms(vg_rel, w, after=()):
    t, cols = vg_rel.shape
    d = w.shape[0]
    n = t // N_TENSOR
    return pl.pallas_call(
        terms_kernel,
        in_specs=[VM, VM] + [ANY] * len(after),
        out_specs=[VM] * N_TENSOR,
        out_shape=[jax.ShapeDtypeStruct((n, d), BF)] * N_TENSOR,
        compiler_params=pltpu.CompilerParams(vmem_limit_bytes=VMEM_LIMIT),
        cost_estimate=SMALL,
        name="row_terms",
    )(vg_rel, w, *after)


def weight_kernel(core_ref, *refs):
    chunks, vgta_ref, vgtb_ref, keep_ref, send_ref = refs[:16], refs[16], refs[17], refs[-2], refs[-1]
    vgt = jnp.concatenate([vgta_ref[...], vgtb_ref[...]], axis=1)
    half, blk = keep_ref.shape[1], keep_ref.shape[2]
    first = core_ref[0] == 0
    for i in range(keep_ref.shape[0]):
        rows = jnp.concatenate([c[:, i * blk:(i + 1) * blk] for c in chunks], axis=0)
        part = jnp.dot(vgt, rows, preferred_element_type=F32).astype(BF)
        keep_ref[i] = jnp.where(first, part[:half], part[half:])
        send_ref[i] = jnp.where(first, part[half:], part[:half])


def weight_terms(core, chunks, vgt_a, vgt_b, after):
    n, d = chunks[0].shape
    cols, t = vgt_a.shape
    shape = jax.ShapeDtypeStruct((N_Z, cols // 2, d // N_Z), BF)
    return pl.pallas_call(
        weight_kernel,
        in_specs=[pl.BlockSpec(memory_space=pltpu.SMEM)] + [VM] * 18 + [ANY] * len(after),
        out_specs=[VM, VM],
        out_shape=[shape, shape],
        compiler_params=pltpu.CompilerParams(vmem_limit_bytes=VMEM_LIMIT),
        cost_estimate=SMALL,
        name="weight_terms",
    )(core, *chunks, vgt_a, vgt_b, *after)


def weight_sum(keep, sent, xl, core, after):
    u = add(keep, other_core(sent), after)
    groups = [[(z * 2 + x) * 2 + c for z in range(N_Z)] for x in range(2) for c in range(2)]
    u = lax.psum_scatter(u, "dp", scatter_dimension=0, axis_index_groups=groups)
    half, lanes = u.shape[0], u.shape[1] // 2
    mine = lax.dynamic_slice_in_dim(u, xl * lanes, lanes, 1).astype(F32)
    theirs = lax.dynamic_slice_in_dim(u, (1 - xl) * lanes, lanes, 1)
    total = (mine + other_xl(theirs).astype(F32)).T
    rows = lanes // 2
    mine = lax.dynamic_slice_in_dim(total, core * rows, rows, 0)
    theirs = other_core(lax.dynamic_slice_in_dim(total, (1 - core) * rows, rows, 0))
    first = core == 0
    return jnp.concatenate(
        [jnp.where(first, mine, theirs), jnp.where(first, theirs, mine)], axis=1)


def shards(tile_rows, queries, keys, w_value, ctx_grad, move, blocks):
    rank_count = lax.axis_size("dp")
    half_ranks = rank_count // 2
    my_rank = lax.axis_index("dp")
    partner = (my_rank + half_ranks) % rank_count
    me = lax.axis_index("tensor").astype(jnp.int32)
    xl, core = (my_rank // 2) % 2, my_rank % 2

    own_dest = move[my_rank]
    live = own_dest[:2] == my_rank * 2 + jnp.arange(2, dtype=jnp.int32)
    leaving = (own_dest[2] >= 0) & (own_dest[2] // 2 == partner)
    sender_dest = move[partner, 2]
    arriving = (sender_dest >= 0) & (sender_dest // 2 == my_rank)
    slot_b = jnp.where(arriving, sender_dest % 2, jnp.where(live[0], 1, 0)).astype(jnp.int32)
    slot_a = 1 - slot_b
    live_a, live_b = live[slot_a], live[slot_b]

    def own(home, slot):
        return lax.dynamic_index_in_dim(home, slot, 0, keepdims=False)

    def kept(home):
        row = own(home, slot_a)
        return jnp.where(live_a, row, jnp.zeros_like(row))

    def second(home, got):
        row = own(home, slot_b)
        return jnp.where(arriving, got, jnp.where(live_b, row, jnp.zeros_like(row)))

    got_rows = to_partner(pack([tile_rows], 2)[0])
    rows_a = gather_chunks(kept(tile_rows), 1, 3)
    rows_b = gather_chunks(second(tile_rows, got_rows), 3, 1)
    got_qk = to_partner(pack([queries, keys], 2, [rows_a[2]]))

    def info(slot, is_live, came):
        return jnp.stack([me, slot, is_live.astype(jnp.int32), came.astype(jnp.int32)])

    values_a = project_values(rows_a, w_value)
    att_a, vg_a, vgt_a, dqk_a = attend(
        info(slot_a, live_a, jnp.zeros((), bool)), queries, keys, values_a, ctx_grad, blocks)
    values_b = project_values(rows_b, w_value)
    terms_a = row_terms(vg_a, w_value, [values_b])
    arrived_a = [swap(terms_a[6], 1), swap(terms_a[2], 3), swap(terms_a[5], 1)]
    att_b, vg_b, vgt_b, dqk_b = attend(
        info(slot_b, live_b, arriving), queries, keys, values_b, ctx_grad, blocks, got_qk,
        [terms_a[0]])
    back_qk = to_partner(dqk_b)
    keep, sent = weight_terms(
        core.astype(jnp.int32).reshape(1), rows_a + rows_b, vgt_a, vgt_b, [])
    terms_b = row_terms(vg_b, w_value, [sent])
    weight_grad = weight_sum(keep, sent, xl, core, [terms_b[0]] + [])

    first_b = scatter_first(terms_b, 3, 1, lambda x, y: x + y)
    next_b = scatter_next(terms_b, first_b, 1)
    late = lambda x, y: add(x, y, [next_b])
    first_a = (late(terms_a[7], arrived_a[0]), late(terms_a[1], arrived_a[1]),
               late(terms_a[4], arrived_a[2]))
    next_a = scatter_next(terms_a, first_a, 3)
    grad_b = scatter_last(terms_b, first_b, next_b, 3, 1)
    grad_a = scatter_last(terms_a, first_a, next_a, 1, 3)

    def by_slot(of_a, of_b):
        first = slot_a == 0
        return [jnp.where(first, of_a, of_b), jnp.where(first, of_b, of_a)]

    def home(of_a, of_b, back):
        here = by_slot(of_a, of_b)
        rows = [jnp.where(live[0], here[0], 0), jnp.where(live[1], here[1], 0),
                jnp.where(leaving, back, 0)]
        return jnp.stack(rows).astype(BF)

    attended = jnp.stack(by_slot(att_a, att_b))
    tile_grad = home(grad_a, grad_b, to_partner(grad_b))
    query_grad = home(dqk_a[0], dqk_b[0], back_qk[0])
    key_grad = home(dqk_a[1], dqk_b[1], back_qk[1])
    return (attended, tile_grad, query_grad, key_grad, weight_grad)


def solution(mesh):
    placed = (
        P("dp", "tensor", None),
        P("dp", None, "tensor"),
        P("dp", None, "tensor"),
        P(None, "tensor"),
        P("dp", None, "tensor"),
        P(),
        P("dp", None),
    )
    return jax.shard_map(
        shards,
        mesh=mesh,
        in_specs=placed,
        out_specs=(
            P("dp", None, "tensor"),
            P("dp", "tensor", None),
            P("dp", None, "tensor"),
            P("dp", None, "tensor"),
            P("dp", "tensor"),
        ),
        check_vma=False,
    )
```

```python
import functools
import math

import jax
import jax.numpy as jnp
from jax import lax
from jax.experimental import pallas as pl
from jax.experimental.pallas import tpu as pltpu
from jax.sharding import PartitionSpec as P

HD = 128
N_TENSOR = 8
N_Z = 8
masked_score = -1e30
BF = jnp.bfloat16
F32 = jnp.float32
VMEM_LIMIT = 10 * 1024 * 1024
BLK = 1024
SMALL = pl.CostEstimate(flops=1, bytes_accessed=1, transcendentals=0)


def swap(x, d):
    return lax.ppermute(x, "tensor", [(i, i ^ d) for i in range(N_TENSOR)])


def dp_perm(x, move):
    pairs = []
    for z in range(N_Z):
        for xl in range(2):
            for c in range(2):
                z2, xl2, c2 = move(z, xl, c)
                pairs.append(((z * 2 + xl) * 2 + c, ((z2 % N_Z) * 2 + xl2 % 2) * 2 + c2 % 2))
    return lax.ppermute(x, "dp", pairs)


def to_partner(x):
    return dp_perm(x, lambda z, xl, c: (z + N_Z // 2, xl, c))


def along_z(x, by):
    return dp_perm(x, lambda z, xl, c: (z + by, xl, c))


def other_core(x):
    return dp_perm(x, lambda z, xl, c: (z, xl, c + 1))


def other_xl(x):
    return dp_perm(x, lambda z, xl, c: (z, xl + 1, c))


def gather_chunks(own, a, b):
    c = [None] * N_TENSOR
    c[0] = own
    c[4] = swap(own, 4)
    c[a] = swap(own, a)
    c[b] = swap(own, b)
    c[4 ^ b] = swap(c[b], 4)
    c[2] = swap(c[a], b)
    c[4 ^ a] = swap(c[4], a)
    c[6] = swap(c[4 ^ b], a)
    return c


def scatter_first(t, a, b, add_up):
    return (add_up(t[4 ^ b], swap(t[6], a)), add_up(t[a], swap(t[2], b)),
            add_up(t[4], swap(t[4 ^ a], a)))


def scatter_next(t, first, b):
    return t[b] + swap(first[0], 4)


def scatter_last(t, first, ub, a, b):
    _, ua, u4 = first
    parts = (t[0], swap(u4, 4), swap(ua, a), swap(ub, b))
    return sum(p.astype(F32) for p in parts).astype(BF)


VM = pl.BlockSpec(memory_space=pltpu.VMEM)
ANY = pl.BlockSpec(memory_space=pl.ANY)


def pack_kernel(n, *refs):
    for i in range(n):
        refs[-1][i] = refs[i][0]


def pack(homes, slot, after=()):
    _, t, cols = homes[0].shape
    n = len(homes)
    last = pl.BlockSpec((1, t, cols), lambda i: (slot, 0, 0))
    return pl.pallas_call(
        functools.partial(pack_kernel, n),
        grid=(1,),
        in_specs=[last] * n + [ANY] * len(after),
        out_specs=pl.BlockSpec((n, t, cols), lambda i: (0, 0, 0)),
        out_shape=jax.ShapeDtypeStruct((n, t, cols), BF),
        compiler_params=pltpu.CompilerParams(vmem_limit_bytes=VMEM_LIMIT),
        cost_estimate=SMALL,
        name="pack",
    )(*homes, *after)


def add_kernel(a_ref, b_ref, *refs):
    refs[-1][...] = a_ref[...] + b_ref[...]


def add(a, b, after):
    flat = a.ndim == 2
    blk = VM if flat else pl.BlockSpec((1,) + a.shape[1:], lambda i: (i, 0, 0))
    return pl.pallas_call(
        add_kernel,
        grid=() if flat else (a.shape[0],),
        in_specs=[blk, blk] + [ANY] * len(after),
        out_specs=blk,
        out_shape=jax.ShapeDtypeStruct(a.shape, a.dtype),
        compiler_params=pltpu.CompilerParams(vmem_limit_bytes=VMEM_LIMIT),
        cost_estimate=SMALL,
        name="add",
    )(a, b, *after)


def sum_kernel(a_ref, b_ref, c_ref, d_ref, *refs):
    parts = (a_ref[...], b_ref[...], c_ref[...], d_ref[...])
    refs[-1][...] = sum(p.astype(F32) for p in parts).astype(BF)


def sum_last(parts, after):
    return pl.pallas_call(
        sum_kernel,
        in_specs=[VM] * 4 + [ANY] * len(after),
        out_specs=VM,
        out_shape=jax.ShapeDtypeStruct(parts[0].shape, BF),
        compiler_params=pltpu.CompilerParams(vmem_limit_bytes=VMEM_LIMIT),
        cost_estimate=SMALL,
        name="sum_last",
    )(*parts, *after)


def value_kernel(*refs):
    chunks, w_ref, out_ref = refs[:8], refs[8], refs[-1]
    d = w_ref.shape[0]
    acc = jnp.zeros(out_ref.shape, F32)
    for at in range(0, d, BLK):
        rows = jnp.concatenate([c[:, at:at + BLK] for c in chunks], axis=0)
        acc += jnp.dot(rows, w_ref[at:at + BLK, :], preferred_element_type=F32)
    out_ref[...] = acc.astype(BF)


def project_values(chunks, w, after=()):
    n, d = chunks[0].shape
    cols = w.shape[1]
    return pl.pallas_call(
        value_kernel,
        in_specs=[VM] * 9 + [ANY] * len(after),
        out_specs=VM,
        out_shape=jax.ShapeDtypeStruct((8 * n, cols), BF),
        compiler_params=pltpu.CompilerParams(vmem_limit_bytes=VMEM_LIMIT),
        cost_estimate=SMALL,
        name="project_values",
    )(*chunks, w, *after)


def attend_kernel(arrived, me_ref, *refs):
    q_ref, k_ref, v_ref, g_ref, bq_ref, bk_ref = refs[:6]
    got_ref = refs[6] if arrived else None
    att_ref, vg_ref, vgt_ref, dqk_ref, v_abs, vg_abs = refs[-6:]
    me, live, came = me_ref[0], me_ref[2] == 1, me_ref[3] == 1
    n = q_ref.shape[0] // N_TENSOR
    scale = 1.0 / math.sqrt(HD)
    for d in range(N_TENSOR):
        at = pl.multiple_of((me ^ d) * n, n)
        v_abs[pl.ds(at, n), :] = v_ref[d * n:(d + 1) * n, :]
    g, v = g_ref[...], v_abs[...]
    q = jnp.where(live, q_ref[...], 0).astype(BF)
    k = jnp.where(live, k_ref[...], 0).astype(BF)
    if arrived:
        q = jnp.where(came, got_ref[0], q)
        k = jnp.where(came, got_ref[1], k)
    nt = (((1,), (1,)), ((), ()))
    tn = (((0,), (0,)), ((), ()))
    s = lax.dot_general(q, k, nt, preferred_element_type=F32) * scale
    s = jnp.where(bq_ref[...] == bk_ref[...], s, masked_score)
    e = jnp.exp(s - jnp.max(s, axis=-1, keepdims=True))
    p = e / jnp.sum(e, axis=-1, keepdims=True)
    low = p.astype(BF)
    att_ref[...] = jnp.dot(low, v, preferred_element_type=F32).astype(BF)
    pg = lax.dot_general(g, v, nt, preferred_element_type=F32)
    vg_abs[...] = lax.dot_general(low, g, tn, preferred_element_type=F32).astype(BF)
    inner = jnp.sum(pg * p, axis=-1, keepdims=True)
    sg = (p * (pg - inner) * scale).astype(BF)
    dqk_ref[0] = jnp.dot(sg, k, preferred_element_type=F32).astype(BF)
    dqk_ref[1] = lax.dot_general(sg, q, tn, preferred_element_type=F32).astype(BF)
    vg = jnp.concatenate(
        [vg_abs[pl.ds(pl.multiple_of((me ^ d) * n, n), n), :] for d in range(N_TENSOR)], axis=0)
    vg_ref[...] = vg
    vgt_ref[...] = vg.T


def attend(info, q_home, k_home, v_rel, g, blocks, got=None, after=()):
    _, t, cols = q_home.shape
    row = pl.BlockSpec((None, t, HD), lambda h, m: (m[1], 0, h))
    flat = pl.BlockSpec((t, HD), lambda h, m: (0, h))
    two = pl.BlockSpec((2, t, HD), lambda h, m: (0, 0, h))
    arrived = got is not None
    shape = jax.ShapeDtypeStruct
    return pl.pallas_call(
        functools.partial(attend_kernel, arrived),
        grid_spec=pltpu.PrefetchScalarGridSpec(
            num_scalar_prefetch=1,
            grid=(cols // HD,),
            in_specs=[row, row, flat, row]
            + [
                pl.BlockSpec((None, t, 1), lambda h, m: (m[1], 0, 0)),
                pl.BlockSpec((None, 1, t), lambda h, m: (m[1], 0, 0)),
            ]
            + [two] * arrived + [ANY] * len(after),
            out_specs=[flat, flat, pl.BlockSpec((HD, t), lambda h, m: (h, 0)), two],
            scratch_shapes=[pltpu.VMEM((t, HD), BF)] * 2,
        ),
        out_shape=[shape((t, cols), BF), shape((t, cols), BF), shape((cols, t), BF),
                   shape((2, t, cols), BF)],
        compiler_params=pltpu.CompilerParams(vmem_limit_bytes=VMEM_LIMIT),
        cost_estimate=SMALL,
        name="attend",
    )(info, q_home, k_home, v_rel, g, blocks[:, :, None], blocks[:, None, :],
      *([got] if arrived else []), *after)


def terms_kernel(vg_ref, w_ref, *refs):
    outs = refs[-N_TENSOR:]
    n = outs[0].shape[0]
    for at in range(0, w_ref.shape[0], BLK):
        part = lax.dot_general(
            vg_ref[...], w_ref[at:at + BLK, :], (((1,), (1,)), ((), ())),
            preferred_element_type=F32,
        ).astype(BF)
        for d in range(N_TENSOR):
            outs[d][:, at:at + BLK] = part[d * n:(d + 1) * n]


def row_terms(vg_rel, w, after=()):
    t, cols = vg_rel.shape
    d = w.shape[0]
    n = t // N_TENSOR
    return pl.pallas_call(
        terms_kernel,
        in_specs=[VM, VM] + [ANY] * len(after),
        out_specs=[VM] * N_TENSOR,
        out_shape=[jax.ShapeDtypeStruct((n, d), BF)] * N_TENSOR,
        compiler_params=pltpu.CompilerParams(vmem_limit_bytes=VMEM_LIMIT),
        cost_estimate=SMALL,
        name="row_terms",
    )(vg_rel, w, *after)


def weight_kernel(core_ref, *refs):
    chunks, vgta_ref, vgtb_ref, keep_ref, send_ref = refs[:16], refs[16], refs[17], refs[-2], refs[-1]
    vgt = jnp.concatenate([vgta_ref[...], vgtb_ref[...]], axis=1)
    half, blk = keep_ref.shape[1], keep_ref.shape[2]
    first = core_ref[0] == 0
    for i in range(keep_ref.shape[0]):
        rows = jnp.concatenate([c[:, i * blk:(i + 1) * blk] for c in chunks], axis=0)
        part = jnp.dot(vgt, rows, preferred_element_type=F32).astype(BF)
        keep_ref[i] = jnp.where(first, part[:half], part[half:])
        send_ref[i] = jnp.where(first, part[half:], part[:half])


def weight_terms(core, chunks, vgt_a, vgt_b, after):
    n, d = chunks[0].shape
    cols, t = vgt_a.shape
    shape = jax.ShapeDtypeStruct((N_Z, cols // 2, d // N_Z), BF)
    return pl.pallas_call(
        weight_kernel,
        in_specs=[pl.BlockSpec(memory_space=pltpu.SMEM)] + [VM] * 18 + [ANY] * len(after),
        out_specs=[VM, VM],
        out_shape=[shape, shape],
        compiler_params=pltpu.CompilerParams(vmem_limit_bytes=2 * VMEM_LIMIT),
        cost_estimate=SMALL,
        name="weight_terms",
    )(core, *chunks, vgt_a, vgt_b, *after)


def over_z(u):
    groups = [[(z * 2 + x) * 2 + c for z in range(N_Z)] for x in range(2) for c in range(2)]
    return lax.psum_scatter(u, "dp", scatter_dimension=0, axis_index_groups=groups)


def weight_sum(u, xl, core):
    half, lanes = u.shape[0], u.shape[1] // 2
    mine = lax.dynamic_slice_in_dim(u, xl * lanes, lanes, 1).astype(F32)
    theirs = lax.dynamic_slice_in_dim(u, (1 - xl) * lanes, lanes, 1)
    total = (mine + other_xl(theirs).astype(F32)).T
    rows = lanes // 2
    mine = lax.dynamic_slice_in_dim(total, core * rows, rows, 0)
    theirs = other_core(lax.dynamic_slice_in_dim(total, (1 - core) * rows, rows, 0))
    first = core == 0
    return jnp.concatenate(
        [jnp.where(first, mine, theirs), jnp.where(first, theirs, mine)], axis=1)


def shards(tile_rows, queries, keys, w_value, ctx_grad, move, blocks):
    rank_count = lax.axis_size("dp")
    half_ranks = rank_count // 2
    my_rank = lax.axis_index("dp")
    partner = (my_rank + half_ranks) % rank_count
    me = lax.axis_index("tensor").astype(jnp.int32)
    xl, core = (my_rank // 2) % 2, my_rank % 2

    own_dest = move[my_rank]
    live = own_dest[:2] == my_rank * 2 + jnp.arange(2, dtype=jnp.int32)
    leaving = (own_dest[2] >= 0) & (own_dest[2] // 2 == partner)
    sender_dest = move[partner, 2]
    arriving = (sender_dest >= 0) & (sender_dest // 2 == my_rank)
    slot_b = jnp.where(arriving, sender_dest % 2, jnp.where(live[0], 1, 0)).astype(jnp.int32)
    slot_a = 1 - slot_b
    live_a, live_b = live[slot_a], live[slot_b]

    def own(home, slot):
        return lax.dynamic_index_in_dim(home, slot, 0, keepdims=False)

    def kept(home):
        row = own(home, slot_a)
        return jnp.where(live_a, row, jnp.zeros_like(row))

    def second(home, got):
        row = own(home, slot_b)
        return jnp.where(arriving, got, jnp.where(live_b, row, jnp.zeros_like(row)))

    got_rows = to_partner(pack([tile_rows], 2)[0])
    rows_a = gather_chunks(kept(tile_rows), 1, 3)
    rows_b = gather_chunks(second(tile_rows, got_rows), 3, 1)
    got_qk = to_partner(pack([queries, keys], 2, [rows_a[2]]))

    def info(slot, is_live, came):
        return jnp.stack([me, slot, is_live.astype(jnp.int32), came.astype(jnp.int32)])

    values_a = project_values(rows_a, w_value)
    att_a, vg_a, vgt_a, dqk_a = attend(
        info(slot_a, live_a, jnp.zeros((), bool)), queries, keys, values_a, ctx_grad, blocks)
    values_b = project_values(rows_b, w_value)
    terms_a = row_terms(vg_a, w_value, [values_b])
    arrived_a = [swap(terms_a[6], 1), swap(terms_a[2], 3), swap(terms_a[5], 1)]
    att_b, vg_b, vgt_b, dqk_b = attend(
        info(slot_b, live_b, arriving), queries, keys, values_b, ctx_grad, blocks, got_qk,
        [terms_a[0]])
    back_qk = to_partner(dqk_b)
    keep, sent = weight_terms(
        core.astype(jnp.int32).reshape(1), rows_a + rows_b, vgt_a, vgt_b, [])
    terms_b = row_terms(vg_b, w_value, [sent])
    both_cores = add(keep, other_core(sent), [terms_b[0]])
    z_sum = over_z(both_cores)
    weight_grad = weight_sum(z_sum, xl, core)

    first_b = scatter_first(terms_b, 3, 1, lambda x, y: add(x, y, [both_cores]))
    next_b = scatter_next(terms_b, first_b, 1)
    grad_b = scatter_last(terms_b, first_b, next_b, 3, 1)
    back_rows = to_partner(grad_b)
    late = lambda x, y: add(x, y, [grad_b])
    first_a = (late(terms_a[7], arrived_a[0]), late(terms_a[1], arrived_a[1]),
               late(terms_a[4], arrived_a[2]))
    next_a = scatter_next(terms_a, first_a, 3)
    last_a = [terms_a[0], swap(first_a[2], 4), swap(first_a[1], 1), swap(next_a, 3)]
    grad_a = sum_last(last_a, [z_sum])

    def by_slot(of_a, of_b):
        first = slot_a == 0
        return [jnp.where(first, of_a, of_b), jnp.where(first, of_b, of_a)]

    def home(of_a, of_b, back):
        here = by_slot(of_a, of_b)
        rows = [jnp.where(live[0], here[0], 0), jnp.where(live[1], here[1], 0),
                jnp.where(leaving, back, 0)]
        return jnp.stack(rows).astype(BF)

    attended = jnp.stack(by_slot(att_a, att_b))
    tile_grad = home(grad_a, grad_b, back_rows)
    query_grad = home(dqk_a[0], dqk_b[0], back_qk[0])
    key_grad = home(dqk_a[1], dqk_b[1], back_qk[1])
    return (attended, tile_grad, query_grad, key_grad, weight_grad)


def solution(mesh):
    placed = (
        P("dp", "tensor", None),
        P("dp", None, "tensor"),
        P("dp", None, "tensor"),
        P(None, "tensor"),
        P("dp", None, "tensor"),
        P(),
        P("dp", None),
    )
    return jax.shard_map(
        shards,
        mesh=mesh,
        in_specs=placed,
        out_specs=(
            P("dp", None, "tensor"),
            P("dp", "tensor", None),
            P("dp", None, "tensor"),
            P("dp", None, "tensor"),
            P("dp", "tensor"),
        ),
        check_vma=False,
    )
```

```python
import functools
import math

import jax
import jax.numpy as jnp
from jax import lax
from jax.experimental import pallas as pl
from jax.experimental.pallas import tpu as pltpu
from jax.sharding import PartitionSpec as P

HD = 128
N_TENSOR = 8
N_Z = 8
masked_score = -1e30
BF = jnp.bfloat16
F32 = jnp.float32
VMEM_LIMIT = 10 * 1024 * 1024
BLK = 1024
SMALL = pl.CostEstimate(flops=1, bytes_accessed=1, transcendentals=0)


def swap(x, d):
    return lax.ppermute(x, "tensor", [(i, i ^ d) for i in range(N_TENSOR)])


def dp_perm(x, move):
    pairs = []
    for z in range(N_Z):
        for xl in range(2):
            for c in range(2):
                z2, xl2, c2 = move(z, xl, c)
                pairs.append(((z * 2 + xl) * 2 + c, ((z2 % N_Z) * 2 + xl2 % 2) * 2 + c2 % 2))
    return lax.ppermute(x, "dp", pairs)


def to_partner(x):
    return dp_perm(x, lambda z, xl, c: (z + N_Z // 2, xl, c))


def along_z(x, by):
    return dp_perm(x, lambda z, xl, c: (z + by, xl, c))


def other_core(x):
    return dp_perm(x, lambda z, xl, c: (z, xl, c + 1))


def other_xl(x):
    return dp_perm(x, lambda z, xl, c: (z, xl + 1, c))


def gather_chunks(own, a, b):
    c = [None] * N_TENSOR
    c[0] = own
    c[4] = swap(own, 4)
    c[a] = swap(own, a)
    c[b] = swap(own, b)
    c[4 ^ b] = swap(c[b], 4)
    c[2] = swap(c[a], b)
    c[4 ^ a] = swap(c[4], a)
    c[6] = swap(c[4 ^ b], a)
    return c


def scatter_first(t, a, b, add_up):
    return (add_up(t[4 ^ b], swap(t[6], a)), add_up(t[a], swap(t[2], b)),
            add_up(t[4], swap(t[4 ^ a], a)))


def scatter_next(t, first, b):
    return t[b] + swap(first[0], 4)


def scatter_last(t, first, ub, a, b):
    _, ua, u4 = first
    parts = (t[0], swap(u4, 4), swap(ua, a), swap(ub, b))
    return sum(p.astype(F32) for p in parts).astype(BF)


VM = pl.BlockSpec(memory_space=pltpu.VMEM)
ANY = pl.BlockSpec(memory_space=pl.ANY)


def pack_kernel(n, *refs):
    for i in range(n):
        refs[-1][i] = refs[i][0]


def pack(homes, slot, after=()):
    _, t, cols = homes[0].shape
    n = len(homes)
    last = pl.BlockSpec((1, t, cols), lambda i: (slot, 0, 0))
    return pl.pallas_call(
        functools.partial(pack_kernel, n),
        grid=(1,),
        in_specs=[last] * n + [ANY] * len(after),
        out_specs=pl.BlockSpec((n, t, cols), lambda i: (0, 0, 0)),
        out_shape=jax.ShapeDtypeStruct((n, t, cols), BF),
        compiler_params=pltpu.CompilerParams(vmem_limit_bytes=VMEM_LIMIT),
        cost_estimate=SMALL,
        name="pack",
    )(*homes, *after)


def add_kernel(a_ref, b_ref, *refs):
    refs[-1][...] = a_ref[...] + b_ref[...]


def add(a, b, after):
    flat = a.ndim == 2
    blk = VM if flat else pl.BlockSpec((1,) + a.shape[1:], lambda i: (i, 0, 0))
    return pl.pallas_call(
        add_kernel,
        grid=() if flat else (a.shape[0],),
        in_specs=[blk, blk] + [ANY] * len(after),
        out_specs=blk,
        out_shape=jax.ShapeDtypeStruct(a.shape, a.dtype),
        compiler_params=pltpu.CompilerParams(vmem_limit_bytes=VMEM_LIMIT),
        cost_estimate=SMALL,
        name="add",
    )(a, b, *after)


def sum_kernel(a_ref, b_ref, c_ref, d_ref, *refs):
    parts = (a_ref[...], b_ref[...], c_ref[...], d_ref[...])
    refs[-1][...] = sum(p.astype(F32) for p in parts).astype(BF)


def sum_last(parts, after):
    return pl.pallas_call(
        sum_kernel,
        in_specs=[VM] * 4 + [ANY] * len(after),
        out_specs=VM,
        out_shape=jax.ShapeDtypeStruct(parts[0].shape, BF),
        compiler_params=pltpu.CompilerParams(vmem_limit_bytes=VMEM_LIMIT),
        cost_estimate=SMALL,
        name="sum_last",
    )(*parts, *after)


def value_kernel(*refs):
    chunks, w_ref, out_ref = refs[:8], refs[8], refs[-1]
    d = w_ref.shape[0]
    acc = jnp.zeros(out_ref.shape, F32)
    for at in range(0, d, BLK):
        rows = jnp.concatenate([c[:, at:at + BLK] for c in chunks], axis=0)
        acc += jnp.dot(rows, w_ref[at:at + BLK, :], preferred_element_type=F32)
    out_ref[...] = acc.astype(BF)


def project_values(chunks, w, after=()):
    n, d = chunks[0].shape
    cols = w.shape[1]
    return pl.pallas_call(
        value_kernel,
        in_specs=[VM] * 9 + [ANY] * len(after),
        out_specs=VM,
        out_shape=jax.ShapeDtypeStruct((8 * n, cols), BF),
        compiler_params=pltpu.CompilerParams(vmem_limit_bytes=VMEM_LIMIT),
        cost_estimate=SMALL,
        name="project_values",
    )(*chunks, w, *after)


def attend_kernel(arrived, me_ref, *refs):
    q_ref, k_ref, v_ref, g_ref, bq_ref, bk_ref = refs[:6]
    got_ref = refs[6] if arrived else None
    att_ref, vg_ref, vgt_ref, dqk_ref, v_abs, vg_abs = refs[-6:]
    me, live, came = me_ref[0], me_ref[2] == 1, me_ref[3] == 1
    n = q_ref.shape[0] // N_TENSOR
    scale = 1.0 / math.sqrt(HD)
    for d in range(N_TENSOR):
        at = pl.multiple_of((me ^ d) * n, n)
        v_abs[pl.ds(at, n), :] = v_ref[d * n:(d + 1) * n, :]
    g, v = g_ref[...], v_abs[...]
    q = jnp.where(live, q_ref[...], 0).astype(BF)
    k = jnp.where(live, k_ref[...], 0).astype(BF)
    if arrived:
        q = jnp.where(came, got_ref[0], q)
        k = jnp.where(came, got_ref[1], k)
    nt = (((1,), (1,)), ((), ()))
    tn = (((0,), (0,)), ((), ()))
    s = lax.dot_general(q, k, nt, preferred_element_type=F32) * scale
    s = jnp.where(bq_ref[...] == bk_ref[...], s, masked_score)
    e = jnp.exp(s - jnp.max(s, axis=-1, keepdims=True))
    p = e / jnp.sum(e, axis=-1, keepdims=True)
    low = p.astype(BF)
    att_ref[...] = jnp.dot(low, v, preferred_element_type=F32).astype(BF)
    pg = lax.dot_general(g, v, nt, preferred_element_type=F32)
    vg_abs[...] = lax.dot_general(low, g, tn, preferred_element_type=F32).astype(BF)
    inner = jnp.sum(pg * p, axis=-1, keepdims=True)
    sg = (p * (pg - inner) * scale).astype(BF)
    dqk_ref[0] = jnp.dot(sg, k, preferred_element_type=F32).astype(BF)
    dqk_ref[1] = lax.dot_general(sg, q, tn, preferred_element_type=F32).astype(BF)
    vg = jnp.concatenate(
        [vg_abs[pl.ds(pl.multiple_of((me ^ d) * n, n), n), :] for d in range(N_TENSOR)], axis=0)
    vg_ref[...] = vg
    vgt_ref[...] = vg.T


def attend(info, q_home, k_home, v_rel, g, blocks, got=None, after=()):
    _, t, cols = q_home.shape
    row = pl.BlockSpec((None, t, HD), lambda h, m: (m[1], 0, h))
    flat = pl.BlockSpec((t, HD), lambda h, m: (0, h))
    two = pl.BlockSpec((2, t, HD), lambda h, m: (0, 0, h))
    arrived = got is not None
    shape = jax.ShapeDtypeStruct
    return pl.pallas_call(
        functools.partial(attend_kernel, arrived),
        grid_spec=pltpu.PrefetchScalarGridSpec(
            num_scalar_prefetch=1,
            grid=(cols // HD,),
            in_specs=[row, row, flat, row]
            + [
                pl.BlockSpec((None, t, 1), lambda h, m: (m[1], 0, 0)),
                pl.BlockSpec((None, 1, t), lambda h, m: (m[1], 0, 0)),
            ]
            + [two] * arrived + [ANY] * len(after),
            out_specs=[flat, flat, pl.BlockSpec((HD, t), lambda h, m: (h, 0)), two],
            scratch_shapes=[pltpu.VMEM((t, HD), BF)] * 2,
        ),
        out_shape=[shape((t, cols), BF), shape((t, cols), BF), shape((cols, t), BF),
                   shape((2, t, cols), BF)],
        compiler_params=pltpu.CompilerParams(vmem_limit_bytes=VMEM_LIMIT),
        cost_estimate=SMALL,
        name="attend",
    )(info, q_home, k_home, v_rel, g, blocks[:, :, None], blocks[:, None, :],
      *([got] if arrived else []), *after)


def terms_kernel(vg_ref, w_ref, *refs):
    outs = refs[-N_TENSOR:]
    n = outs[0].shape[0]
    for at in range(0, w_ref.shape[0], BLK):
        part = lax.dot_general(
            vg_ref[...], w_ref[at:at + BLK, :], (((1,), (1,)), ((), ())),
            preferred_element_type=F32,
        ).astype(BF)
        for d in range(N_TENSOR):
            outs[d][:, at:at + BLK] = part[d * n:(d + 1) * n]


def row_terms(vg_rel, w, after=()):
    t, cols = vg_rel.shape
    d = w.shape[0]
    n = t // N_TENSOR
    return pl.pallas_call(
        terms_kernel,
        in_specs=[VM, VM] + [ANY] * len(after),
        out_specs=[VM] * N_TENSOR,
        out_shape=[jax.ShapeDtypeStruct((n, d), BF)] * N_TENSOR,
        compiler_params=pltpu.CompilerParams(vmem_limit_bytes=VMEM_LIMIT),
        cost_estimate=SMALL,
        name="row_terms",
    )(vg_rel, w, *after)


def weight_kernel(core_ref, *refs):
    chunks, vgta_ref, vgtb_ref, keep_ref, send_ref = refs[:16], refs[16], refs[17], refs[-2], refs[-1]
    vgt = jnp.concatenate([vgta_ref[...], vgtb_ref[...]], axis=1)
    half, blk = keep_ref.shape[1], keep_ref.shape[2]
    first = core_ref[0] == 0
    for i in range(keep_ref.shape[0]):
        rows = jnp.concatenate([c[:, i * blk:(i + 1) * blk] for c in chunks], axis=0)
        part = jnp.dot(vgt, rows, preferred_element_type=F32).astype(BF)
        keep_ref[i] = jnp.where(first, part[:half], part[half:])
        send_ref[i] = jnp.where(first, part[half:], part[:half])


def weight_terms(core, chunks, vgt_a, vgt_b, after):
    n, d = chunks[0].shape
    cols, t = vgt_a.shape
    shape = jax.ShapeDtypeStruct((N_Z, cols // 2, d // N_Z), BF)
    return pl.pallas_call(
        weight_kernel,
        in_specs=[pl.BlockSpec(memory_space=pltpu.SMEM)] + [VM] * 18 + [ANY] * len(after),
        out_specs=[VM, VM],
        out_shape=[shape, shape],
        compiler_params=pltpu.CompilerParams(vmem_limit_bytes=2 * VMEM_LIMIT),
        cost_estimate=SMALL,
        name="weight_terms",
    )(core, *chunks, vgt_a, vgt_b, *after)


def over_z(u):
    groups = [[(z * 2 + x) * 2 + c for z in range(N_Z)] for x in range(2) for c in range(2)]
    return lax.psum_scatter(u, "dp", scatter_dimension=0, axis_index_groups=groups)


def weight_sum(u, xl, core):
    half, lanes = u.shape[0], u.shape[1] // 2
    mine = lax.dynamic_slice_in_dim(u, xl * lanes, lanes, 1).astype(F32)
    theirs = lax.dynamic_slice_in_dim(u, (1 - xl) * lanes, lanes, 1)
    total = (mine + other_xl(theirs).astype(F32)).T
    rows = lanes // 2
    mine = lax.dynamic_slice_in_dim(total, core * rows, rows, 0)
    theirs = other_core(lax.dynamic_slice_in_dim(total, (1 - core) * rows, rows, 0))
    first = core == 0
    return jnp.concatenate(
        [jnp.where(first, mine, theirs), jnp.where(first, theirs, mine)], axis=1)


def shards(tile_rows, queries, keys, w_value, ctx_grad, move, blocks):
    rank_count = lax.axis_size("dp")
    half_ranks = rank_count // 2
    my_rank = lax.axis_index("dp")
    partner = (my_rank + half_ranks) % rank_count
    me = lax.axis_index("tensor").astype(jnp.int32)
    xl, core = (my_rank // 2) % 2, my_rank % 2

    own_dest = move[my_rank]
    live = own_dest[:2] == my_rank * 2 + jnp.arange(2, dtype=jnp.int32)
    leaving = (own_dest[2] >= 0) & (own_dest[2] // 2 == partner)
    sender_dest = move[partner, 2]
    arriving = (sender_dest >= 0) & (sender_dest // 2 == my_rank)
    slot_b = jnp.where(arriving, sender_dest % 2, jnp.where(live[0], 1, 0)).astype(jnp.int32)
    slot_a = 1 - slot_b
    live_a, live_b = live[slot_a], live[slot_b]

    def own(home, slot):
        return lax.dynamic_index_in_dim(home, slot, 0, keepdims=False)

    def kept(home):
        row = own(home, slot_a)
        return jnp.where(live_a, row, jnp.zeros_like(row))

    def second(home, got):
        row = own(home, slot_b)
        return jnp.where(arriving, got, jnp.where(live_b, row, jnp.zeros_like(row)))

    got_rows = to_partner(pack([tile_rows], 2)[0])
    rows_a = gather_chunks(kept(tile_rows), 1, 3)
    rows_b = gather_chunks(second(tile_rows, got_rows), 3, 1)
    got_qk = to_partner(pack([queries, keys], 2, [rows_a[2]]))

    def info(slot, is_live, came):
        return jnp.stack([me, slot, is_live.astype(jnp.int32), came.astype(jnp.int32)])

    values_a = project_values(rows_a, w_value)
    att_a, vg_a, vgt_a, dqk_a = attend(
        info(slot_a, live_a, jnp.zeros((), bool)), queries, keys, values_a, ctx_grad, blocks)
    values_b = project_values(rows_b, w_value)
    terms_a = row_terms(vg_a, w_value, [values_b])
    arrived_a = [swap(terms_a[6], 1), swap(terms_a[2], 3), swap(terms_a[5], 1)]
    att_b, vg_b, vgt_b, dqk_b = attend(
        info(slot_b, live_b, arriving), queries, keys, values_b, ctx_grad, blocks, got_qk,
        [terms_a[0]])
    back_qk = to_partner(dqk_b)
    keep, sent = weight_terms(
        core.astype(jnp.int32).reshape(1), rows_a + rows_b, vgt_a, vgt_b, [])
    terms_b = row_terms(vg_b, w_value, [sent])
    both_cores = add(keep, other_core(sent), [terms_b[0]])
    z_sum = over_z(both_cores)
    weight_grad = weight_sum(z_sum, xl, core)

    first_b = scatter_first(terms_b, 3, 1, lambda x, y: add(x, y, [both_cores]))
    next_b = scatter_next(terms_b, first_b, 1)
    grad_b = scatter_last(terms_b, first_b, next_b, 3, 1)
    back_rows = to_partner(grad_b)
    late = lambda x, y: add(x, y, [grad_b])
    first_a = (late(terms_a[7], arrived_a[0]), late(terms_a[1], arrived_a[1]),
               late(terms_a[4], arrived_a[2]))
    next_a = scatter_next(terms_a, first_a, 3)
    last_a = [terms_a[0], swap(first_a[2], 4), swap(first_a[1], 1), swap(next_a, 3)]
    grad_a = sum_last(last_a, [z_sum, back_rows])

    def by_slot(of_a, of_b):
        first = slot_a == 0
        return [jnp.where(first, of_a, of_b), jnp.where(first, of_b, of_a)]

    def home(of_a, of_b, back):
        here = by_slot(of_a, of_b)
        rows = [jnp.where(live[0], here[0], 0), jnp.where(live[1], here[1], 0),
                jnp.where(leaving, back, 0)]
        return jnp.stack(rows).astype(BF)

    attended = jnp.stack(by_slot(att_a, att_b))
    tile_grad = home(grad_a, grad_b, back_rows)
    query_grad = home(dqk_a[0], dqk_b[0], back_qk[0])
    key_grad = home(dqk_a[1], dqk_b[1], back_qk[1])
    return (attended, tile_grad, query_grad, key_grad, weight_grad)


def solution(mesh):
    placed = (
        P("dp", "tensor", None),
        P("dp", None, "tensor"),
        P("dp", None, "tensor"),
        P(None, "tensor"),
        P("dp", None, "tensor"),
        P(),
        P("dp", None),
    )
    return jax.shard_map(
        shards,
        mesh=mesh,
        in_specs=placed,
        out_specs=(
            P("dp", None, "tensor"),
            P("dp", "tensor", None),
            P("dp", None, "tensor"),
            P("dp", None, "tensor"),
            P("dp", "tensor"),
        ),
        check_vma=False,
    )
```
